32 devices in a mesh: dp: 2 (over core), blk: 4 (over y, x), head: 4 (over z).
Axes of the slice: x: 2, y: 2, z: 4, core: 2. Of those that a mesh axis runs over, the one named last changes fastest.
Arguments:
- queries: bfloat16 [2, 2048, 4096], P('dp', ('blk', 'head')), may hold values from -8 to 8
- keys: bfloat16 [2, 2048, 512], P('dp', ('blk', 'head')), may hold values from -8 to 8
- values: bfloat16 [2, 2048, 512], P('dp', ('blk', 'head')), may hold values from -6 to 6
- lengths: int32 [2, 48], P('dp'), may hold values from 1 to 128, 2048 in all within a row
Outputs:
- attended: bfloat16 [2, 2048, 4096], P('dp', ('blk', 'head'))
The draws below stay inside these ranges and needn't reach their ends.
Inputs may be any that keep to these rules, and one draw needn't show every extreme that they name: `lengths`: each row sums to 2048; the longest document has exactly 128 positions.
All inputs are finite; a program needn't handle non-finite values.
Results may differ from the reference program's by a relative error of at most 0.0035.
Values may be sent and summed in bfloat16 or wider, within the bound.
A program may use at most 64 MiB of HBM per device.

```python
import math
import jax
import jax.numpy as jnp
import numpy as np
from jax import lax

HEAD_DIM = 128
Q_HEADS = 32
KV_HEADS = 4
NDOC = 48
SEQS = 2
LEN = 2048
BLOCK = 512
DOC_MOST = 128
REACH = 1
QW = 4096
KW = 512


def draw_queries(key, part):
    base = jnp.clip(jax.random.normal(jax.random.fold_in(key, 1), (SEQS, LEN, QW), jnp.float32), -4.0, 4.0)
    return base.astype(jnp.bfloat16)


def draw_keys(key, part):
    base = jnp.clip(jax.random.normal(jax.random.fold_in(key, 2), (SEQS, LEN, KW), jnp.float32), -4.0, 4.0)
    return base.astype(jnp.bfloat16)


def block_scale(key, shape, split, least, high):
    gain, own = 1.0, jax.random.fold_in(key, 6)
    for axis_at, shards_of in split:
        draws = jnp.exp(jax.random.uniform(jax.random.fold_in(own, axis_at), (shards_of,), jnp.float32, least / len(split), high / len(split)))
        gain = gain * jnp.repeat(draws, shape[axis_at] // shards_of).reshape([-1 if axis == axis_at else 1 for axis in range(len(shape))])
    return gain


def length_profile(amount, total, bound, skew):
    loads = [(1 << 20) // math.isqrt(rank ** skew) + 1 for rank in range(2, amount + 1)]
    spare, given = total - bound - (amount - 1), [1] * (amount - 1)
    while spare > 0:
        movable = [i for i in range(amount - 1) if given[i] < bound]
        whole, budget = sum([loads[i] for i in movable]), spare
        for i in movable:
            more = min(bound - given[i], max(1, budget * loads[i] // whole), spare)
            given[i] = given[i] + more
            spare = spare - more
    return np.array([bound] + given)


def ragged_sizes(key, number_of, total, most, slope):
    if number_of == 2:
        one = jax.random.randint(key, (), max(1, total - most), min(most, total - 1) + 1)
        return jnp.stack([one, total - one])
    tallies = jnp.asarray(length_profile(number_of, total, most, slope), jnp.int32)
    couples = (number_of - 1) // 2
    source_of, receiver = tallies[1:1 + 2 * couples:2], tallies[2:2 + 2 * couples:2]
    slack = jnp.minimum(source_of - 1, most - receiver)
    passed = jax.random.randint(jax.random.fold_in(key, 1), (couples,), 0, 1 << 20) % (slack + 1)
    tallies = tallies.at[1:1 + 2 * couples:2].set(source_of - passed).at[2:2 + 2 * couples:2].set(receiver + passed)
    return tallies[jax.random.permutation(jax.random.fold_in(key, 2), number_of)]


def scatter_about(rng, shape, spread, limit, pieces=(), held_as=jnp.bfloat16):
    values = spread * jax.random.normal(rng, shape, jnp.float32)
    if pieces:
        values = values * block_scale(rng, shape, pieces, -0.22, 0.18)
    return jnp.clip(values, -limit, limit).astype(held_as)


def setup_inputs(seed: int = 0) -> dict:
    seeds = jax.random.split(jax.random.key(seed), 5)
    return {
        "queries": draw_queries(jax.random.fold_in(seeds[4], 71), 0),
        "keys": draw_keys(jax.random.fold_in(seeds[4], 71), 0),
        "values": scatter_about(seeds[2], (SEQS, LEN, KW), 1.0, 6.0, ((0, 2), (1, 16))),
        "lengths": jax.vmap(lambda own: ragged_sizes(own, NDOC, LEN, DOC_MOST, 2))(jax.random.split(seeds[3], SEQS)).reshape((SEQS, NDOC)).astype(jnp.int32),
    }


def one_sequence(operands):
    query_all, key_all, value_all, doc_lengths = operands
    ends = jnp.cumsum(doc_lengths).astype(jnp.int32)
    group = Q_HEADS // KV_HEADS
    front = REACH * BLOCK
    key_pad = jnp.concatenate([jnp.zeros((front, KW), key_all.dtype), key_all], axis=0)
    value_pad = jnp.concatenate([jnp.zeros((front, KW), value_all.dtype), value_all], axis=0)
    count = LEN // BLOCK
    span = (REACH + 1) * BLOCK

    def doc_of(pos):
        return lax.optimization_barrier(jnp.sum((pos[:, None] >= ends[None, :]).astype(jnp.int32), axis=1))

    def one_block(index):
        start = (index * BLOCK).astype(jnp.int32)
        qs = lax.dynamic_slice_in_dim(query_all, start, BLOCK, 0)
        ks = lax.dynamic_slice_in_dim(key_pad, start, span, 0)
        vs = lax.dynamic_slice_in_dim(value_pad, start, span, 0)
        q_pos = start + jnp.arange(BLOCK, dtype=jnp.int32)
        k_pos = start - front + jnp.arange(span, dtype=jnp.int32)
        allowed = (doc_of(q_pos)[:, None] == doc_of(k_pos)[None, :]) & (k_pos[None, :] <= q_pos[:, None]) & (k_pos[None, :] >= 0)
        q4 = qs.reshape(BLOCK, KV_HEADS, group, HEAD_DIM).astype(jnp.float32)
        k3 = ks.reshape(span, KV_HEADS, HEAD_DIM).astype(jnp.float32)
        v3 = vs.reshape(span, KV_HEADS, HEAD_DIM).astype(jnp.float32)
        scores = jnp.einsum('qhgd,khd->hgqk', q4, k3) / jnp.sqrt(jnp.float32(HEAD_DIM))
        scores = jnp.where(allowed, scores, jnp.float32(-1e+30))
        top = lax.optimization_barrier(jnp.max(scores, axis=-1, keepdims=True))
        expo = jnp.exp(scores - top)
        total = lax.optimization_barrier(jnp.sum(expo, axis=-1))
        weight = expo.astype(jnp.bfloat16).astype(jnp.float32)
        summed = jnp.einsum('hgqk,khd->qhgd', weight, v3)
        result = summed / jnp.transpose(total, (2, 0, 1))[..., None]
        return result.reshape(BLOCK, QW).astype(jnp.bfloat16)
    blocks = lax.map(one_block, jnp.arange(count, dtype=jnp.int32))
    return blocks.reshape(LEN, QW)

def reference(queries, keys, values, lengths):
    return lax.map(one_sequence, (queries, keys, values, lengths))
```

```python
import functools
import math

import jax
import jax.numpy as jnp
from jax import lax
from jax.experimental import pallas as pl
from jax.experimental.pallas import tpu as pltpu
from jax.sharding import PartitionSpec as P

HEAD_DIM = 128
MESH = pl.DeviceIdType.MESH
MASKED = -1e30


def kernel(
    sizes, len_ref, q_hbm, k_hbm, v_hbm, out_ref,
    q_buf, k_own, k_far, v_all, own_scores, weights,
    load_sem, send_sem, recv_sem,
):
    blks, heads, near, rows, kv_count, group = sizes
    spread = blks * heads
    place = lax.axis_index("blk") * heads + lax.axis_index("head")

    def at(index):
        index = lax.rem(index + spread, spread)
        return {"blk": lax.div(index, heads), "head": lax.rem(index, heads)}

    def cols(h):
        return pl.ds(h * HEAD_DIM, HEAD_DIM)

    barrier = pltpu.get_barrier_semaphore()
    for offset in range(1, near + 1):
        pl.semaphore_signal(barrier, inc=1, device_id=at(place - offset), device_id_type=MESH)

    load_k = pltpu.make_async_copy(k_hbm.at[0], k_own, load_sem.at[0])
    load_q = pltpu.make_async_copy(q_hbm.at[0], q_buf, load_sem.at[1])
    load_v = [
        pltpu.make_async_copy(
            v_hbm.at[0, :, cols(h)], v_all.at[h, pl.ds(0, rows), pl.ds(0, HEAD_DIM)], load_sem.at[2 + h]
        )
        for h in range(kv_count)
    ]
    pl.semaphore_wait(barrier, near)

    def remote(offset, what, h):
        if what == 0:
            src, dst = k_hbm.at[0, :, cols(h)], k_far.at[h, pl.ds((offset - 1) * rows, rows), :]
        else:
            src = v_hbm.at[0, :, cols(h)]
            dst = v_all.at[h, pl.ds(offset * rows, rows), pl.ds(0, HEAD_DIM)]
        return pltpu.make_async_remote_copy(
            src_ref=src,
            dst_ref=dst,
            send_sem=send_sem.at[offset - 1, what, h],
            recv_sem=recv_sem.at[offset - 1, what, h],
            device_id=at(place + offset),
            device_id_type=MESH,
        )

    copies = {
        (offset, what, h): remote(offset, what, h)
        for what in range(2)
        for h in range(kv_count)
        for offset in range(1, near + 1)
    }
    for copy in copies.values():
        copy.start()
    load_k.start()
    load_q.start()
    for copy in load_v:
        copy.start()

    docs = len_ref.shape[1]
    row = lax.broadcasted_iota(jnp.int32, (docs, docs), 0)
    col = lax.broadcasted_iota(jnp.int32, (docs, docs), 1)
    down = jnp.sum(jnp.where(row == col, len_ref[...], 0), axis=1, keepdims=True)
    ends = jnp.sum(jnp.where(row <= col, down, 0), axis=0, keepdims=True)
    q_pos = place * rows + lax.broadcasted_iota(jnp.int32, (rows, 1), 0)
    first = jnp.max(jnp.where(ends <= q_pos, ends, 0), axis=1, keepdims=True)
    lane = lax.broadcasted_iota(jnp.int32, (rows, rows), 1)
    own_pos = place * rows + lane
    own_bias = jnp.where((own_pos >= first) & (own_pos <= q_pos), 0.0, MASKED)
    far_bias = jnp.concatenate(
        [jnp.where(own_pos - offset * rows >= first, 0.0, MASKED) for offset in range(1, near + 1)], axis=1
    )

    v_all[:, :, HEAD_DIM:] = jnp.ones((kv_count, (near + 1) * rows, HEAD_DIM), v_all.dtype)

    def scores_of(j, keys):
        return lax.dot_general(
            q_buf[:, cols(j)], keys, (((1,), (1,)), ((), ())), preferred_element_type=jnp.float32
        )

    load_k.wait()
    load_q.wait()
    for j in range(kv_count * group):
        own_scores[j] = scores_of(j, k_own[:, cols(j // group)]) + own_bias

    change = math.log2(math.e) / math.sqrt(HEAD_DIM)
    for h in range(kv_count):
        for offset in range(1, near + 1):
            copies[offset, 0, h].wait_recv()
        for j in range(h * group, (h + 1) * group):
            own = own_scores[j]
            far = scores_of(j, k_far[h]) + far_bias
            top = jnp.maximum(jnp.max(own, axis=1, keepdims=True), jnp.max(far, axis=1, keepdims=True))
            weights[j, :, :rows] = jnp.exp2((own - top) * change).astype(weights.dtype)
            weights[j, :, rows:] = jnp.exp2((far - top) * change).astype(weights.dtype)

    for h in range(kv_count):
        load_v[h].wait()
        for offset in range(1, near + 1):
            copies[offset, 1, h].wait_recv()
        for j in range(h * group, (h + 1) * group):
            summed = jnp.dot(weights[j], v_all[h], preferred_element_type=jnp.float32)
            out_ref[0, :, cols(j)] = (summed[:, :HEAD_DIM] / summed[:, HEAD_DIM:]).astype(out_ref.dtype)

    for copy in copies.values():
        copy.wait_send()


def solution(mesh):
    blks, heads = mesh.shape["blk"], mesh.shape["head"]

    def on_device(queries, keys, values, lengths):
        rows = queries.shape[1]
        kv_count = keys.shape[2] // HEAD_DIM
        group = queries.shape[2] // keys.shape[2]
        doc_most = rows * blks * heads // 16
        near = (doc_most - 1) // rows + 1
        span = (near + 1) * rows
        work = 4 * rows * span * queries.shape[2]
        return pl.pallas_call(
            functools.partial(kernel, (blks, heads, near, rows, kv_count, group)),
            out_shape=jax.ShapeDtypeStruct(queries.shape, queries.dtype),
            in_specs=[pl.BlockSpec(memory_space=pltpu.VMEM)] + [pl.BlockSpec(memory_space=pltpu.HBM)] * 3,
            out_specs=pl.BlockSpec(memory_space=pltpu.VMEM),
            scratch_shapes=[
                pltpu.VMEM(queries.shape[1:], queries.dtype),
                pltpu.VMEM(keys.shape[1:], keys.dtype),
                pltpu.VMEM((kv_count, near * rows, HEAD_DIM), keys.dtype),
                pltpu.VMEM((kv_count, span, 2 * HEAD_DIM), values.dtype),
                pltpu.VMEM((kv_count * group, rows, rows), jnp.float32),
                pltpu.VMEM((kv_count * group, rows, span), jnp.bfloat16),
                pltpu.SemaphoreType.DMA((2 + kv_count,)),
                pltpu.SemaphoreType.DMA((near, 2, kv_count)),
                pltpu.SemaphoreType.DMA((near, 2, kv_count)),
            ],
            compiler_params=pltpu.CompilerParams(
                collective_id=0, has_side_effects=True, vmem_limit_bytes=40 * 2**20
            ),
            cost_estimate=pl.CostEstimate(
                flops=work, bytes_accessed=4 * queries.size, transcendentals=work // (4 * HEAD_DIM)
            ),
        )(lengths, queries, keys, values)

    return jax.shard_map(
        on_device,
        mesh=mesh,
        in_specs=(
            P("dp", ("blk", "head"), None),
            P("dp", ("blk", "head"), None),
            P("dp", ("blk", "head"), None),
            P("dp", None),
        ),
        out_specs=P("dp", ("blk", "head"), None),
        check_vma=False,
    )
```

```python
import functools
import math

import jax
import jax.numpy as jnp
from jax import lax
from jax.experimental import pallas as pl
from jax.experimental.pallas import tpu as pltpu
from jax.sharding import PartitionSpec as P

HEAD_DIM = 128
MESH = pl.DeviceIdType.MESH
MASKED = -1e30


def kernel(
    sizes, len_hbm, q_hbm, k_hbm, v_hbm, out_hbm,
    len_ref, q_buf, k_own, k_far, v_all, own_scores, weights, out_buf,
    load_sem, send_sem, recv_sem, out_sem,
):
    blks, heads, near, rows, kv_count, group = sizes
    spread = blks * heads
    place = lax.axis_index("blk") * heads + lax.axis_index("head")

    def at(index):
        return {"blk": lax.div(index, heads), "head": lax.rem(index, heads)}

    def cols(h):
        return pl.ds(h * HEAD_DIM, HEAD_DIM)

    barrier = pltpu.get_barrier_semaphore()
    for offset in range(1, near + 1):

        @pl.when(place >= offset)
        def _():
            pl.semaphore_signal(barrier, inc=1, device_id=at(place - offset), device_id_type=MESH)

    load_k = pltpu.make_async_copy(k_hbm.at[0], k_own, load_sem.at[0])
    load_q = pltpu.make_async_copy(q_hbm.at[0], q_buf, load_sem.at[1])
    load_len = pltpu.make_async_copy(len_hbm, len_ref, load_sem.at[2 + kv_count])
    load_v = [
        pltpu.make_async_copy(
            v_hbm.at[0, :, cols(h)], v_all.at[h, pl.ds(0, rows), pl.ds(0, HEAD_DIM)], load_sem.at[2 + h]
        )
        for h in range(kv_count)
    ]
    load_len.start()
    load_k.start()
    load_q.start()
    for copy in load_v:
        copy.start()

    @pl.when(place < spread - 1)
    def _():
        pl.semaphore_wait(barrier, jnp.minimum(spread - 1 - place, near))

    def remote(offset, what, h):
        if what == 0:
            src, dst = k_hbm.at[0, :, cols(h)], k_far.at[h, pl.ds((offset - 1) * rows, rows), :]
        else:
            src = v_hbm.at[0, :, cols(h)]
            dst = v_all.at[h, pl.ds(offset * rows, rows), pl.ds(0, HEAD_DIM)]
        return pltpu.make_async_remote_copy(
            src_ref=src,
            dst_ref=dst,
            send_sem=send_sem.at[offset - 1, what, h],
            recv_sem=recv_sem.at[offset - 1, what, h],
            device_id=at(place + offset),
            device_id_type=MESH,
        )

    pieces = [(what, h) for what in range(2) for h in range(kv_count)]
    for offset in range(1, near + 1):

        @pl.when(place + offset < spread)
        def _():
            for piece in pieces:
                remote(offset, *piece).start()

        @pl.when(place < offset)
        def _():
            k_far[:, (offset - 1) * rows : offset * rows, :] = jnp.zeros((kv_count, rows, HEAD_DIM), k_far.dtype)
            v_all[:, offset * rows : (offset + 1) * rows, :HEAD_DIM] = jnp.zeros(
                (kv_count, rows, HEAD_DIM), v_all.dtype
            )

    def arrived(what, h):
        for offset in range(1, near + 1):

            @pl.when(place >= offset)
            def _():
                remote(offset, what, h).wait_recv()

    load_len.wait()
    docs = len_ref.shape[1]
    row = lax.broadcasted_iota(jnp.int32, (docs, docs), 0)
    col = lax.broadcasted_iota(jnp.int32, (docs, docs), 1)
    down = jnp.sum(jnp.where(row == col, len_ref[...], 0), axis=1, keepdims=True)
    ends = jnp.sum(jnp.where(row <= col, down, 0), axis=0, keepdims=True)
    q_pos = place * rows + lax.broadcasted_iota(jnp.int32, (rows, 1), 0)
    first = jnp.max(jnp.where(ends <= q_pos, ends, 0), axis=1, keepdims=True)
    lane = lax.broadcasted_iota(jnp.int32, (rows, rows), 1)
    own_pos = place * rows + lane
    own_bias = jnp.where((own_pos >= first) & (own_pos <= q_pos), 0.0, MASKED)
    far_bias = jnp.concatenate(
        [jnp.where(own_pos - offset * rows >= first, 0.0, MASKED) for offset in range(1, near + 1)], axis=1
    )

    v_all[:, :, HEAD_DIM:] = jnp.ones((kv_count, (near + 1) * rows, HEAD_DIM), v_all.dtype)

    half = group // 2

    def store(i):
        part = pl.ds(i * half * HEAD_DIM, half * HEAD_DIM)
        return pltpu.make_async_copy(out_buf.at[:, part], out_hbm.at[0, :, part], out_sem.at[i])

    def scores_of(j, keys):
        return lax.dot_general(
            q_buf[:, cols(j)], keys, (((1,), (1,)), ((), ())), preferred_element_type=jnp.float32
        )

    load_k.wait()
    load_q.wait()
    for j in range(kv_count * group):
        own_scores[j] = scores_of(j, k_own[:, cols(j // group)]) + own_bias

    change = math.log2(math.e) / math.sqrt(HEAD_DIM)
    for h in range(kv_count):
        arrived(0, h)
        for j in range(h * group, (h + 1) * group):
            own = own_scores[j]
            far = scores_of(j, k_far[h]) + far_bias
            top = jnp.maximum(jnp.max(own, axis=1, keepdims=True), jnp.max(far, axis=1, keepdims=True))
            weights[j, :, :rows] = jnp.exp2((own - top) * change).astype(weights.dtype)
            weights[j, :, rows:] = jnp.exp2((far - top) * change).astype(weights.dtype)

    for h in range(kv_count):
        load_v[h].wait()
        arrived(1, h)
        for j in range(h * group, (h + 1) * group):
            summed = jnp.dot(weights[j], v_all[h], preferred_element_type=jnp.float32)
            out_buf[:, cols(j)] = (summed[:, :HEAD_DIM] / summed[:, HEAD_DIM:]).astype(out_buf.dtype)
            if (j + 1) % half == 0:
                store(j // half).start()

    for offset in range(1, near + 1):

        @pl.when(place + offset < spread)
        def _():
            for piece in pieces:
                remote(offset, *piece).wait_send()

    for i in range(2 * kv_count):
        store(i).wait()


def solution(mesh):
    blks, heads = mesh.shape["blk"], mesh.shape["head"]

    def on_device(queries, keys, values, lengths):
        rows = queries.shape[1]
        kv_count = keys.shape[2] // HEAD_DIM
        group = queries.shape[2] // keys.shape[2]
        doc_most = rows * blks * heads // 16
        near = (doc_most - 1) // rows + 1
        span = (near + 1) * rows
        work = 4 * rows * span * queries.shape[2]
        return pl.pallas_call(
            functools.partial(kernel, (blks, heads, near, rows, kv_count, group)),
            out_shape=jax.ShapeDtypeStruct(queries.shape, queries.dtype),
            in_specs=[pl.BlockSpec(memory_space=pl.ANY)] * 4,
            out_specs=pl.BlockSpec(memory_space=pl.ANY),
            scratch_shapes=[
                pltpu.VMEM(lengths.shape, lengths.dtype),
                pltpu.VMEM(queries.shape[1:], queries.dtype),
                pltpu.VMEM(keys.shape[1:], keys.dtype),
                pltpu.VMEM((kv_count, near * rows, HEAD_DIM), keys.dtype),
                pltpu.VMEM((kv_count, span, 2 * HEAD_DIM), values.dtype),
                pltpu.VMEM((kv_count * group, rows, rows), jnp.float32),
                pltpu.VMEM((kv_count * group, rows, span), jnp.bfloat16),
                pltpu.VMEM(queries.shape[1:], queries.dtype),
                pltpu.SemaphoreType.DMA((3 + kv_count,)),
                pltpu.SemaphoreType.DMA((near, 2, kv_count)),
                pltpu.SemaphoreType.DMA((near, 2, kv_count)),
                pltpu.SemaphoreType.DMA((2 * kv_count,)),
            ],
            compiler_params=pltpu.CompilerParams(
                collective_id=0, has_side_effects=True, vmem_limit_bytes=60 * 2**20
            ),
            cost_estimate=pl.CostEstimate(
                flops=work, bytes_accessed=4 * queries.size, transcendentals=work // (4 * HEAD_DIM)
            ),
        )(lengths, queries, keys, values)

    return jax.shard_map(
        on_device,
        mesh=mesh,
        in_specs=(
            P("dp", ("blk", "head"), None),
            P("dp", ("blk", "head"), None),
            P("dp", ("blk", "head"), None),
            P("dp", None),
        ),
        out_specs=P("dp", ("blk", "head"), None),
        check_vma=False,
    )
```

```python
import functools
import math

import jax
import jax.numpy as jnp
from jax import lax
from jax.experimental import pallas as pl
from jax.experimental.pallas import tpu as pltpu
from jax.sharding import PartitionSpec as P

HEAD_DIM = 128
MESH = pl.DeviceIdType.MESH
MASKED = -1e30


def kernel(
    sizes, len_hbm, q_hbm, k_hbm, v_hbm, *refs
):
    (
    *out, len_ref, q_buf, k_own, k_far, v_all, own_scores, weights, out_buf,
    load_sem, send_sem, recv_sem, out_sem,
    ) = refs
    blks, heads, near, rows, kv_count, group = sizes
    spread = blks * heads
    place = lax.axis_index("blk") * heads + lax.axis_index("head")

    def at(index):
        return {"blk": lax.div(index, heads), "head": lax.rem(index, heads)}

    def cols(h):
        return pl.ds(h * HEAD_DIM, HEAD_DIM)

    barrier = pltpu.get_barrier_semaphore()
    for offset in range(1, near + 1):

        @pl.when(place >= offset)
        def _():
            pl.semaphore_signal(barrier, inc=1, device_id=at(place - offset), device_id_type=MESH)

    load_k = pltpu.make_async_copy(k_hbm.at[0], k_own, load_sem.at[0])
    load_q = pltpu.make_async_copy(q_hbm.at[0], q_buf, load_sem.at[1])
    load_len = pltpu.make_async_copy(len_hbm, len_ref, load_sem.at[2 + kv_count])
    load_v = [
        pltpu.make_async_copy(
            v_hbm.at[0, :, cols(h)], v_all.at[h, pl.ds(0, rows), pl.ds(0, HEAD_DIM)], load_sem.at[2 + h]
        )
        for h in range(kv_count)
    ]
    load_len.start()
    load_k.start()
    load_q.start()
    for copy in load_v:
        copy.start()

    @pl.when(place < spread - 1)
    def _():
        pl.semaphore_wait(barrier, jnp.minimum(spread - 1 - place, near))

    def remote(offset, what, h):
        if what == 0:
            src, dst = k_hbm.at[0, :, cols(h)], k_far.at[h, pl.ds((offset - 1) * rows, rows), :]
        else:
            src = v_hbm.at[0, :, cols(h)]
            dst = v_all.at[h, pl.ds(offset * rows, rows), pl.ds(0, HEAD_DIM)]
        return pltpu.make_async_remote_copy(
            src_ref=src,
            dst_ref=dst,
            send_sem=send_sem.at[offset - 1, what, h],
            recv_sem=recv_sem.at[offset - 1, what, h],
            device_id=at(place + offset),
            device_id_type=MESH,
        )

    pieces = [(what, h) for what in range(2) for h in range(kv_count)]
    for offset in range(1, near + 1):

        @pl.when(place + offset < spread)
        def _():
            for piece in pieces:
                remote(offset, *piece).start()

        @pl.when(place < offset)
        def _():
            k_far[:, (offset - 1) * rows : offset * rows, :] = jnp.zeros((kv_count, rows, HEAD_DIM), k_far.dtype)
            v_all[:, offset * rows : (offset + 1) * rows, :HEAD_DIM] = jnp.zeros(
                (kv_count, rows, HEAD_DIM), v_all.dtype
            )

    def arrived(what, h):
        for offset in range(1, near + 1):

            @pl.when(place >= offset)
            def _():
                remote(offset, what, h).wait_recv()

    load_len.wait()
    docs = len_ref.shape[1]
    row = lax.broadcasted_iota(jnp.int32, (docs, docs), 0)
    col = lax.broadcasted_iota(jnp.int32, (docs, docs), 1)
    down = jnp.sum(jnp.where(row == col, len_ref[...], 0), axis=1, keepdims=True)
    ends = jnp.sum(jnp.where(row <= col, down, 0), axis=0, keepdims=True)
    q_pos = place * rows + lax.broadcasted_iota(jnp.int32, (rows, 1), 0)
    first = jnp.max(jnp.where(ends <= q_pos, ends, 0), axis=1, keepdims=True)
    lane = lax.broadcasted_iota(jnp.int32, (rows, rows), 1)
    own_pos = place * rows + lane
    own_bias = jnp.where((own_pos >= first) & (own_pos <= q_pos), 0.0, MASKED)
    far_bias = jnp.concatenate(
        [jnp.where(own_pos - offset * rows >= first, 0.0, MASKED) for offset in range(1, near + 1)], axis=1
    )

    v_all[:, :, HEAD_DIM:] = jnp.ones((kv_count, (near + 1) * rows, HEAD_DIM), v_all.dtype)

    half = group // 2

    def store(i):
        part = pl.ds(i * half * HEAD_DIM, half * HEAD_DIM)
        return pltpu.make_async_copy(out_buf.at[:, part], out[i], out_sem.at[i])

    def scores_of(j, keys):
        return lax.dot_general(
            q_buf[:, cols(j)], keys, (((1,), (1,)), ((), ())), preferred_element_type=jnp.float32
        )

    load_k.wait()
    load_q.wait()
    for j in range(kv_count * group):
        own_scores[j] = scores_of(j, k_own[:, cols(j // group)]) + own_bias

    change = math.log2(math.e) / math.sqrt(HEAD_DIM)
    for h in range(kv_count):
        arrived(0, h)
        for j in range(h * group, (h + 1) * group):
            own = own_scores[j]
            far = scores_of(j, k_far[h]) + far_bias
            top = jnp.maximum(jnp.max(own, axis=1, keepdims=True), jnp.max(far, axis=1, keepdims=True))
            weights[j, :, :rows] = jnp.exp2((own - top) * change).astype(weights.dtype)
            weights[j, :, rows:] = jnp.exp2((far - top) * change).astype(weights.dtype)

    for h in range(kv_count):
        load_v[h].wait()
        arrived(1, h)
        for j in range(h * group, (h + 1) * group):
            summed = jnp.dot(weights[j], v_all[h], preferred_element_type=jnp.float32)
            out_buf[:, cols(j)] = (summed[:, :HEAD_DIM] / summed[:, HEAD_DIM:]).astype(out_buf.dtype)
            if (j + 1) % half == 0:
                store(j // half).start()

    for offset in range(1, near + 1):

        @pl.when(place + offset < spread)
        def _():
            for piece in pieces:
                remote(offset, *piece).wait_send()

    for i in range(2 * kv_count):
        store(i).wait()


def hand_on(*refs):
    *parts, out, sem = refs
    width = parts[0].shape[1]
    copies = [
        pltpu.make_async_copy(part, out.at[0, :, pl.ds(i * width, width)], sem.at[i]) for i, part in enumerate(parts)
    ]
    for copy in copies:
        copy.start()
    for copy in copies:
        copy.wait()


def solution(mesh):
    blks, heads = mesh.shape["blk"], mesh.shape["head"]

    def on_device(queries, keys, values, lengths):
        rows = queries.shape[1]
        kv_count = keys.shape[2] // HEAD_DIM
        group = queries.shape[2] // keys.shape[2]
        doc_most = rows * blks * heads // 16
        near = (doc_most - 1) // rows + 1
        span = (near + 1) * rows
        work = 4 * rows * span * queries.shape[2]
        pieces = 2 * kv_count
        width = queries.shape[2] // pieces
        parts = pl.pallas_call(
            functools.partial(kernel, (blks, heads, near, rows, kv_count, group)),
            out_shape=[jax.ShapeDtypeStruct((rows, width), queries.dtype)] * pieces,
            in_specs=[pl.BlockSpec(memory_space=pl.ANY)] * 4,
            out_specs=[pl.BlockSpec(memory_space=pl.ANY)] * pieces,
            scratch_shapes=[
                pltpu.VMEM(lengths.shape, lengths.dtype),
                pltpu.VMEM(queries.shape[1:], queries.dtype),
                pltpu.VMEM(keys.shape[1:], keys.dtype),
                pltpu.VMEM((kv_count, near * rows, HEAD_DIM), keys.dtype),
                pltpu.VMEM((kv_count, span, 2 * HEAD_DIM), values.dtype),
                pltpu.VMEM((kv_count * group, rows, rows), jnp.float32),
                pltpu.VMEM((kv_count * group, rows, span), jnp.bfloat16),
                pltpu.VMEM(queries.shape[1:], queries.dtype),
                pltpu.SemaphoreType.DMA((3 + kv_count,)),
                pltpu.SemaphoreType.DMA((near, 2, kv_count)),
                pltpu.SemaphoreType.DMA((near, 2, kv_count)),
                pltpu.SemaphoreType.DMA((2 * kv_count,)),
            ],
            compiler_params=pltpu.CompilerParams(
                collective_id=0, has_side_effects=True, vmem_limit_bytes=60 * 2**20
            ),
            cost_estimate=pl.CostEstimate(
                flops=work, bytes_accessed=4 * queries.size, transcendentals=work // (4 * HEAD_DIM)
            ),
        )(lengths, queries, keys, values)
        return pl.pallas_call(
            hand_on,
            out_shape=jax.ShapeDtypeStruct(queries.shape, queries.dtype),
            in_specs=[pl.BlockSpec(memory_space=pl.ANY)] * pieces,
            out_specs=pl.BlockSpec(memory_space=pl.ANY),
            scratch_shapes=[pltpu.SemaphoreType.DMA((pieces,))],
            cost_estimate=pl.CostEstimate(flops=0, bytes_accessed=4 * queries.size, transcendentals=0),
        )(*parts)

    return jax.shard_map(
        on_device,
        mesh=mesh,
        in_specs=(
            P("dp", ("blk", "head"), None),
            P("dp", ("blk", "head"), None),
            P("dp", ("blk", "head"), None),
            P("dp", None),
        ),
        out_specs=P("dp", ("blk", "head"), None),
        check_vma=False,
    )
```

```python
import functools
import math

import jax
import jax.numpy as jnp
from jax import lax
from jax.experimental import pallas as pl
from jax.experimental.pallas import tpu as pltpu
from jax.sharding import PartitionSpec as P

HEAD_DIM = 128
MESH = pl.DeviceIdType.MESH
MASKED = -1e30


def kernel(
    sizes, len_hbm, q_hbm, k_hbm, v_hbm, *refs
):
    (
    *out, len_ref, q_buf, k_own, k_far, v_all, own_scores, weights,
    load_sem, send_sem, recv_sem,
    ) = refs
    blks, heads, near, rows, kv_count, group = sizes
    spread = blks * heads
    place = lax.axis_index("blk") * heads + lax.axis_index("head")

    def at(index):
        return {"blk": lax.div(index, heads), "head": lax.rem(index, heads)}

    def cols(h):
        return pl.ds(h * HEAD_DIM, HEAD_DIM)

    barrier = pltpu.get_barrier_semaphore()
    for offset in range(1, near + 1):

        @pl.when(place >= offset)
        def _():
            pl.semaphore_signal(barrier, inc=1, device_id=at(place - offset), device_id_type=MESH)

    load_k = pltpu.make_async_copy(k_hbm.at[0], k_own, load_sem.at[0])
    load_q = pltpu.make_async_copy(q_hbm.at[0], q_buf, load_sem.at[1])
    load_len = pltpu.make_async_copy(len_hbm, len_ref, load_sem.at[2 + kv_count])
    load_v = [
        pltpu.make_async_copy(
            v_hbm.at[0, :, cols(h)], v_all.at[h, pl.ds(0, rows), pl.ds(0, HEAD_DIM)], load_sem.at[2 + h]
        )
        for h in range(kv_count)
    ]
    load_len.start()
    load_k.start()
    load_q.start()
    for copy in load_v:
        copy.start()

    @pl.when(place < spread - 1)
    def _():
        pl.semaphore_wait(barrier, jnp.minimum(spread - 1 - place, near))

    def remote(offset, what, h):
        if what == 0:
            src, dst = k_hbm.at[0, :, cols(h)], k_far.at[h, pl.ds((offset - 1) * rows, rows), :]
        else:
            src = v_hbm.at[0, :, cols(h)]
            dst = v_all.at[h, pl.ds(offset * rows, rows), pl.ds(0, HEAD_DIM)]
        return pltpu.make_async_remote_copy(
            src_ref=src,
            dst_ref=dst,
            send_sem=send_sem.at[offset - 1, what, h],
            recv_sem=recv_sem.at[offset - 1, what, h],
            device_id=at(place + offset),
            device_id_type=MESH,
        )

    pieces = [(what, h) for what in range(2) for h in range(kv_count)]
    for offset in range(1, near + 1):

        @pl.when(place + offset < spread)
        def _():
            for piece in pieces:
                remote(offset, *piece).start()

        @pl.when(place < offset)
        def _():
            k_far[:, (offset - 1) * rows : offset * rows, :] = jnp.zeros((kv_count, rows, HEAD_DIM), k_far.dtype)
            v_all[:, offset * rows : (offset + 1) * rows, :HEAD_DIM] = jnp.zeros(
                (kv_count, rows, HEAD_DIM), v_all.dtype
            )

    def arrived(what, h):
        for offset in range(1, near + 1):

            @pl.when(place >= offset)
            def _():
                remote(offset, what, h).wait_recv()

    load_len.wait()
    docs = len_ref.shape[1]
    row = lax.broadcasted_iota(jnp.int32, (docs, docs), 0)
    col = lax.broadcasted_iota(jnp.int32, (docs, docs), 1)
    down = jnp.sum(jnp.where(row == col, len_ref[...], 0), axis=1, keepdims=True)
    ends = jnp.sum(jnp.where(row <= col, down, 0), axis=0, keepdims=True)
    q_pos = place * rows + lax.broadcasted_iota(jnp.int32, (rows, 1), 0)
    first = jnp.max(jnp.where(ends <= q_pos, ends, 0), axis=1, keepdims=True)
    lane = lax.broadcasted_iota(jnp.int32, (rows, rows), 1)
    own_pos = place * rows + lane
    own_bias = jnp.where((own_pos >= first) & (own_pos <= q_pos), 0.0, MASKED)
    far_bias = jnp.concatenate(
        [jnp.where(own_pos - offset * rows >= first, 0.0, MASKED) for offset in range(1, near + 1)], axis=1
    )

    v_all[:, :, HEAD_DIM:] = jnp.ones((kv_count, (near + 1) * rows, HEAD_DIM), v_all.dtype)

    half = group // 2

    def scores_of(j, keys):
        return lax.dot_general(
            q_buf[:, cols(j)], keys, (((1,), (1,)), ((), ())), preferred_element_type=jnp.float32
        )

    load_k.wait()
    load_q.wait()
    for j in range(kv_count * group):
        own_scores[j] = scores_of(j, k_own[:, cols(j // group)]) + own_bias

    change = math.log2(math.e) / math.sqrt(HEAD_DIM)
    for h in range(kv_count):
        arrived(0, h)
        for j in range(h * group, (h + 1) * group):
            own = own_scores[j]
            far = scores_of(j, k_far[h]) + far_bias
            top = jnp.maximum(jnp.max(own, axis=1, keepdims=True), jnp.max(far, axis=1, keepdims=True))
            weights[j, :, :rows] = jnp.exp2((own - top) * change).astype(weights.dtype)
            weights[j, :, rows:] = jnp.exp2((far - top) * change).astype(weights.dtype)

    for h in range(kv_count):
        load_v[h].wait()
        arrived(1, h)
        for j in range(h * group, (h + 1) * group):
            summed = jnp.dot(weights[j], v_all[h], preferred_element_type=jnp.float32)
            out[j // half][:, cols(j % half)] = (summed[:, :HEAD_DIM] / summed[:, HEAD_DIM:]).astype(out[0].dtype)

    for offset in range(1, near + 1):

        @pl.when(place + offset < spread)
        def _():
            for piece in pieces:
                remote(offset, *piece).wait_send()


def hand_on(*refs):
    *parts, out, sem = refs
    width = parts[0].shape[1]
    copies = [
        pltpu.make_async_copy(part, out.at[0, :, pl.ds(i * width, width)], sem.at[i]) for i, part in enumerate(parts)
    ]
    for copy in copies:
        copy.start()
    for copy in copies:
        copy.wait()


def solution(mesh):
    blks, heads = mesh.shape["blk"], mesh.shape["head"]

    def on_device(queries, keys, values, lengths):
        rows = queries.shape[1]
        kv_count = keys.shape[2] // HEAD_DIM
        group = queries.shape[2] // keys.shape[2]
        doc_most = rows * blks * heads // 16
        near = (doc_most - 1) // rows + 1
        span = (near + 1) * rows
        work = 4 * rows * span * queries.shape[2]
        pieces = 2 * kv_count
        width = queries.shape[2] // pieces
        parts = pl.pallas_call(
            functools.partial(kernel, (blks, heads, near, rows, kv_count, group)),
            out_shape=[jax.ShapeDtypeStruct((rows, width), queries.dtype)] * pieces,
            in_specs=[pl.BlockSpec(memory_space=pl.ANY)] * 4,
            out_specs=[pl.BlockSpec(memory_space=pltpu.VMEM)] * pieces,
            scratch_shapes=[
                pltpu.VMEM(lengths.shape, lengths.dtype),
                pltpu.VMEM(queries.shape[1:], queries.dtype),
                pltpu.VMEM(keys.shape[1:], keys.dtype),
                pltpu.VMEM((kv_count, near * rows, HEAD_DIM), keys.dtype),
                pltpu.VMEM((kv_count, span, 2 * HEAD_DIM), values.dtype),
                pltpu.VMEM((kv_count * group, rows, rows), jnp.float32),
                pltpu.VMEM((kv_count * group, rows, span), jnp.bfloat16),
                pltpu.SemaphoreType.DMA((3 + kv_count,)),
                pltpu.SemaphoreType.DMA((near, 2, kv_count)),
                pltpu.SemaphoreType.DMA((near, 2, kv_count)),
            ],
            compiler_params=pltpu.CompilerParams(
                collective_id=0, has_side_effects=True, vmem_limit_bytes=55440000
            ),
            cost_estimate=pl.CostEstimate(
                flops=work, bytes_accessed=4 * queries.size, transcendentals=work // (4 * HEAD_DIM)
            ),
        )(lengths, queries, keys, values)
        return pl.pallas_call(
            hand_on,
            out_shape=jax.ShapeDtypeStruct(queries.shape, queries.dtype),
            in_specs=[pl.BlockSpec(memory_space=pltpu.VMEM)] * pieces,
            out_specs=pl.BlockSpec(memory_space=pl.ANY),
            scratch_shapes=[pltpu.SemaphoreType.DMA((pieces,))],
            compiler_params=pltpu.CompilerParams(has_side_effects=False, vmem_limit_bytes=4 * 2**20),
            cost_estimate=pl.CostEstimate(flops=0, bytes_accessed=4 * queries.size, transcendentals=0),
        )(*parts)

    return jax.shard_map(
        on_device,
        mesh=mesh,
        in_specs=(
            P("dp", ("blk", "head"), None),
            P("dp", ("blk", "head"), None),
            P("dp", ("blk", "head"), None),
            P("dp", None),
        ),
        out_specs=P("dp", ("blk", "head"), None),
        check_vma=False,
    )
```

```python
import functools
import math

import jax
import jax.numpy as jnp
from jax import lax
from jax.experimental import pallas as pl
from jax.experimental.pallas import tpu as pltpu
from jax.sharding import PartitionSpec as P

HEAD_DIM = 128
MESH = pl.DeviceIdType.MESH
MASKED = -1e30


def kernel(
    sizes, len_hbm, q_hbm, k_hbm, v_hbm, *refs
):
    (
    *out, len_ref, q_buf, k_own, k_far, v_all, own_scores, weights,
    load_sem, send_sem, recv_sem,
    ) = refs
    blks, heads, near, rows, kv_count, group = sizes
    spread = blks * heads
    place = lax.axis_index("blk") * heads + lax.axis_index("head")

    def at(index):
        return {"blk": lax.div(index, heads), "head": lax.rem(index, heads)}

    def cols(h):
        return pl.ds(h * HEAD_DIM, HEAD_DIM)

    barrier = pltpu.get_barrier_semaphore()
    for offset in range(1, near + 1):

        @pl.when(place >= offset)
        def _():
            pl.semaphore_signal(barrier, inc=1, device_id=at(place - offset), device_id_type=MESH)

    load_k = pltpu.make_async_copy(k_hbm.at[0], k_own, load_sem.at[0])
    load_q = pltpu.make_async_copy(q_hbm.at[0], q_buf, load_sem.at[1])
    load_len = pltpu.make_async_copy(len_hbm, len_ref, load_sem.at[2 + kv_count])
    load_v = [
        pltpu.make_async_copy(
            v_hbm.at[0, :, cols(h)], v_all.at[h, pl.ds(0, rows), pl.ds(0, HEAD_DIM)], load_sem.at[2 + h]
        )
        for h in range(kv_count)
    ]
    load_len.start()
    load_k.start()
    load_q.start()
    for copy in load_v:
        copy.start()

    @pl.when(place < spread - 1)
    def _():
        pl.semaphore_wait(barrier, jnp.minimum(spread - 1 - place, near))

    def remote(offset, what, h):
        if what == 0:
            src, dst = k_hbm.at[0, :, cols(h)], k_far.at[h, pl.ds((offset - 1) * rows, rows), :]
        else:
            src = v_hbm.at[0, :, cols(h)]
            dst = v_all.at[h, pl.ds(offset * rows, rows), pl.ds(0, HEAD_DIM)]
        return pltpu.make_async_remote_copy(
            src_ref=src,
            dst_ref=dst,
            send_sem=send_sem.at[offset - 1, what, h],
            recv_sem=recv_sem.at[offset - 1, what, h],
            device_id=at(place + offset),
            device_id_type=MESH,
        )

    pieces = [(what, h) for what in range(2) for h in range(kv_count)]
    for offset in range(1, near + 1):

        @pl.when(place + offset < spread)
        def _():
            for piece in pieces:
                remote(offset, *piece).start()

        @pl.when(place < offset)
        def _():
            k_far[:, (offset - 1) * rows : offset * rows, :] = jnp.zeros((kv_count, rows, HEAD_DIM), k_far.dtype)
            v_all[:, offset * rows : (offset + 1) * rows, :HEAD_DIM] = jnp.zeros(
                (kv_count, rows, HEAD_DIM), v_all.dtype
            )

    def arrived(what, h):
        for offset in range(1, near + 1):

            @pl.when(place >= offset)
            def _():
                remote(offset, what, h).wait_recv()

    load_len.wait()
    docs = len_ref.shape[1]
    row = lax.broadcasted_iota(jnp.int32, (docs, docs), 0)
    col = lax.broadcasted_iota(jnp.int32, (docs, docs), 1)
    down = jnp.sum(jnp.where(row == col, len_ref[...], 0), axis=1, keepdims=True)
    ends = jnp.sum(jnp.where(row <= col, down, 0), axis=0, keepdims=True)
    q_pos = place * rows + lax.broadcasted_iota(jnp.int32, (rows, 1), 0)
    first = jnp.max(jnp.where(ends <= q_pos, ends, 0), axis=1, keepdims=True)
    lane = lax.broadcasted_iota(jnp.int32, (rows, rows), 1)
    own_pos = place * rows + lane
    own_bias = jnp.where((own_pos >= first) & (own_pos <= q_pos), 0.0, MASKED)
    far_bias = jnp.concatenate(
        [jnp.where(own_pos - offset * rows >= first, 0.0, MASKED) for offset in range(1, near + 1)], axis=1
    )

    v_all[:, :, HEAD_DIM:] = jnp.ones((kv_count, (near + 1) * rows, HEAD_DIM), v_all.dtype)

    half = group // 2

    def scores_of(j, keys):
        return lax.dot_general(
            q_buf[:, cols(j)], keys, (((1,), (1,)), ((), ())), preferred_element_type=jnp.float32
        )

    load_k.wait()
    load_q.wait()
    for j in range(kv_count * group):
        own_scores[j] = scores_of(j, k_own[:, cols(j // group)]) + own_bias

    change = math.log2(math.e) / math.sqrt(HEAD_DIM)
    for h in range(kv_count):
        arrived(0, h)
        for j in range(h * group, (h + 1) * group):
            own = own_scores[j]
            far = scores_of(j, k_far[h]) + far_bias
            top = jnp.maximum(jnp.max(own, axis=1, keepdims=True), jnp.max(far, axis=1, keepdims=True))
            weights[j, :, :rows] = jnp.exp2((own - top) * change).astype(weights.dtype)
            weights[j, :, rows:] = jnp.exp2((far - top) * change).astype(weights.dtype)

    for h in range(kv_count):
        load_v[h].wait()
        arrived(1, h)
        for j in range(h * group, (h + 1) * group):
            summed = jnp.dot(weights[j], v_all[h], preferred_element_type=jnp.float32)
            out[j // half][:, cols(j % half)] = (summed[:, :HEAD_DIM] / summed[:, HEAD_DIM:]).astype(out[0].dtype)

    for offset in range(1, near + 1):

        @pl.when(place + offset < spread)
        def _():
            for piece in pieces:
                remote(offset, *piece).wait_send()


def hand_on(*refs):
    *parts, out, sem = refs
    width = parts[0].shape[1]
    half = parts[0].shape[0] // 2
    copies = [
        pltpu.make_async_copy(
            part.at[pl.ds(r * half, half), :],
            out.at[0, pl.ds(r * half, half), pl.ds(i * width, width)],
            sem.at[2 * i + r],
        )
        for i, part in enumerate(parts)
        for r in range(2)
    ]
    for copy in copies:
        copy.start()
    for copy in copies:
        copy.wait()


def solution(mesh):
    blks, heads = mesh.shape["blk"], mesh.shape["head"]

    def on_device(queries, keys, values, lengths):
        rows = queries.shape[1]
        kv_count = keys.shape[2] // HEAD_DIM
        group = queries.shape[2] // keys.shape[2]
        doc_most = rows * blks * heads // 16
        near = (doc_most - 1) // rows + 1
        span = (near + 1) * rows
        work = 4 * rows * span * queries.shape[2]
        pieces = 2 * kv_count
        width = queries.shape[2] // pieces
        parts = pl.pallas_call(
            functools.partial(kernel, (blks, heads, near, rows, kv_count, group)),
            out_shape=[jax.ShapeDtypeStruct((rows, width), queries.dtype)] * pieces,
            in_specs=[pl.BlockSpec(memory_space=pl.ANY)] * 4,
            out_specs=[pl.BlockSpec(memory_space=pltpu.VMEM)] * pieces,
            scratch_shapes=[
                pltpu.VMEM(lengths.shape, lengths.dtype),
                pltpu.VMEM(queries.shape[1:], queries.dtype),
                pltpu.VMEM(keys.shape[1:], keys.dtype),
                pltpu.VMEM((kv_count, near * rows, HEAD_DIM), keys.dtype),
                pltpu.VMEM((kv_count, span, 2 * HEAD_DIM), values.dtype),
                pltpu.VMEM((kv_count * group, rows, rows), jnp.float32),
                pltpu.VMEM((kv_count * group, rows, span), jnp.bfloat16),
                pltpu.SemaphoreType.DMA((3 + kv_count,)),
                pltpu.SemaphoreType.DMA((near, 2, kv_count)),
                pltpu.SemaphoreType.DMA((near, 2, kv_count)),
            ],
            compiler_params=pltpu.CompilerParams(
                collective_id=0, has_side_effects=True, vmem_limit_bytes=55440000
            ),
            cost_estimate=pl.CostEstimate(
                flops=work, bytes_accessed=4 * queries.size, transcendentals=work // (4 * HEAD_DIM)
            ),
        )(lengths, queries, keys, values)
        return pl.pallas_call(
            hand_on,
            out_shape=jax.ShapeDtypeStruct(queries.shape, queries.dtype),
            in_specs=[pl.BlockSpec(memory_space=pltpu.VMEM)] * pieces,
            out_specs=pl.BlockSpec(memory_space=pl.ANY),
            scratch_shapes=[pltpu.SemaphoreType.DMA((2 * pieces,))],
            compiler_params=pltpu.CompilerParams(has_side_effects=False, vmem_limit_bytes=4 * 2**20),
            cost_estimate=pl.CostEstimate(flops=0, bytes_accessed=4 * queries.size, transcendentals=0),
        )(*parts)

    return jax.shard_map(
        on_device,
        mesh=mesh,
        in_specs=(
            P("dp", ("blk", "head"), None),
            P("dp", ("blk", "head"), None),
            P("dp", ("blk", "head"), None),
            P("dp", None),
        ),
        out_specs=P("dp", ("blk", "head"), None),
        check_vma=False,
    )
```
